512 devices in a mesh: dp: 32 (over y_lo, z), mp: 16 (over x, y_hi, core).
Axes of the slice: x: 4, y: 4 (y_hi: 2, y_lo: 2; y = y_hi * 2 + y_lo), z: 16, core: 2. Of those that a mesh axis runs over, the one named last changes fastest.
Arguments:
- tokens_home: bfloat16 [49152, 4608], P('dp', 'mp'), may hold values from -7 to 7
- q_weight: bfloat16 [4608, 2048], P(None, 'mp'), may hold values from -2 to 2
- kv_weight: bfloat16 [4608, 2048], P(None, 'mp'), may hold values from -2 to 2
- pair_tokens: int32 [128, 2], replicated, may hold values from 1 to 383, as said below
- pair_target: int32 [128], replicated, may hold values from 0 to 31, as said below
- margins: float32 [128], replicated, may hold values from -20 to 20
- grad_attended: bfloat16 [16384, 2048], P('dp', 'mp'), may hold values from -48 to 48
Outputs:
- attended: bfloat16 [16384, 2048], P('dp', 'mp')
- grad_home: bfloat16 [49152, 4608], P('dp', 'mp')
The draws below stay inside these ranges and needn't reach their ends.
Inputs may be any that keep to these rules, and one draw needn't show every extreme that they name: `pair_tokens`: each pair has 1 or more chosen and 1 or more rejected tokens and at most 384 tokens in all; the pairs of one home replica hold at most 1536 tokens together, and the pairs processed by one replica hold exactly 512 tokens together. `pair_target`: replica s sends exactly one of its 4 pairs to each of the replicas s, s + 1, ..., s + 3, counted modulo the number of replicas; which of its pairs goes where varies.
All inputs are finite; a program needn't handle non-finite values.
Results may differ from the reference program's by a relative error of at most 0.022.
Values may be sent and summed in bfloat16 or wider, within the bound.
No kernel may reach another device: no remote copies, remote signals or barrier semaphores. Data moves between devices by JAX's collectives and lax.ppermute only.
A program may use at most 64 MiB of HBM per device.

```python
import jax
import jax.numpy as jnp
from jax import lax

D = 4608
HEAD = 128
SPREAD = 4
RECV = 512
CAP = 384
HOME = 1536
HEADS = 16
PAIRS_ALL = 128
N_DP = 32


def pair_layout(key):
    replicas = PAIRS_ALL // SPREAD
    star_home = jax.random.randint(jax.random.fold_in(key, 101), (), 0, replicas)
    shares = jax.random.randint(jax.random.fold_in(key, 102), (replicas, SPREAD), 1, 4)
    random_spot = jax.random.randint(jax.random.fold_in(key, 103), (replicas,), 0, SPREAD)
    dest_ids = jnp.arange(replicas, dtype=jnp.int32)
    slot_ids = jnp.arange(SPREAD, dtype=jnp.int32)
    gap_star = jnp.mod(dest_ids - star_home, replicas)
    near_star = gap_star < SPREAD
    big_spot = jnp.where(near_star, gap_star, random_spot)
    big_slot = near_star[:, None] & (slot_ids[None, :] == big_spot[:, None])
    share_used = jnp.where(big_slot, 0, shares)
    remain = jnp.where(near_star, RECV - CAP - 2 * (SPREAD - 1), RECV - 2 * SPREAD)
    portion = remain[:, None] * share_used // jnp.sum(share_used, axis=1, keepdims=True)
    leftover = remain - jnp.sum(portion, axis=1)
    first_free = jnp.where(near_star & (big_spot == 0), 1, 0)
    extra_tokens = jnp.where(slot_ids[None, :] == first_free[:, None], leftover[:, None], 0)
    arrival = jnp.where(big_slot, CAP, 2 + portion + extra_tokens)
    order_keys = jax.random.randint(jax.random.fold_in(key, 104), (replicas, SPREAD), 0, 1 << 20) * SPREAD + slot_ids[None, :]
    order_of = jnp.argsort(order_keys, axis=1).astype(jnp.int32)
    pair_target = jnp.mod(dest_ids[:, None] + order_of, replicas)
    totals = arrival[pair_target, order_of]
    chosen = jax.random.randint(jax.random.fold_in(key, 105), (replicas, SPREAD), 1, totals)
    widest = (dest_ids[:, None] == star_home) & (order_of == 0)
    chosen = jnp.where(widest, CAP - 1, chosen)
    pair_tokens = jnp.stack([chosen, totals - chosen], axis=-1).reshape(replicas * SPREAD, 2)
    return (pair_tokens.astype(jnp.int32), pair_target.reshape(replicas * SPREAD).astype(jnp.int32))


def shared_direction(key):
    sign_bits = jax.random.randint(jax.random.fold_in(key, 201), (D,), 0, 2)
    direction = (2 * sign_bits - 1).astype(jnp.float32) / jnp.sqrt(jnp.float32(D))
    group_dirs = jnp.clip(jax.random.normal(jax.random.fold_in(key, 202), (HEADS // 2, HEAD), jnp.float32), -4.0, 4.0)
    return (direction, group_dirs)


def draw_pair_tokens(key, part):
    return pair_layout(key)[0]


def draw_pair_target(key, part):
    return pair_layout(key)[1]


def draw_tokens_home(key, part):
    direction, group_dirs = shared_direction(key)
    key = jax.random.fold_in(key, 13)
    rows_all = PAIRS_ALL // SPREAD * HOME
    planted = jax.random.randint(jax.random.fold_in(key, 1), (rows_all,), 0, 8) == 0
    base = jnp.clip(jax.random.normal(jax.random.fold_in(key, 2), (rows_all, D), jnp.float32), -6.0, 6.0)
    amplitude = jax.random.uniform(jax.random.fold_in(key, 3), (rows_all,), jnp.float32, 2.5, 6.0)
    lift = jnp.where(planted, amplitude, 0.0)
    return (base + lift[:, None] * direction[None, :]).astype(jnp.bfloat16)


def draw_q_weight(key, part):
    direction, group_dirs = shared_direction(key)
    key = jax.random.fold_in(key, 11)
    base = jnp.clip(jax.random.normal(key, (D, HEADS * HEAD), jnp.float32), -6.0, 6.0)
    strength = (20.0 / HEAD) ** 0.5
    columns = jnp.repeat(group_dirs, 2, axis=0).reshape(HEADS * HEAD)
    return (base / jnp.sqrt(jnp.float32(D)) + strength * direction[:, None] * columns[None, :]).astype(jnp.bfloat16)


def draw_kv_weight(key, part):
    direction, group_dirs = shared_direction(key)
    key = jax.random.fold_in(key, 12)
    base = jnp.clip(jax.random.normal(key, (D, HEADS * HEAD), jnp.float32), -6.0, 6.0)
    strength = (20.0 / HEAD) ** 0.5
    columns = jnp.stack([group_dirs, jnp.zeros_like(group_dirs)], axis=1).reshape(HEADS * HEAD)
    return (base / jnp.sqrt(jnp.float32(D)) + strength * direction[:, None] * columns[None, :]).astype(jnp.bfloat16)


def block_levels(key, dims, shards, low, largest):
    def one(dim, shards_of):
        draws = jax.random.uniform(jax.random.fold_in(jax.random.fold_in(key, 6), dim), (shards_of,), jnp.float32, low / len(shards), largest / len(shards))
        return jnp.repeat(jnp.exp(draws), dims[dim] // shards_of).reshape((-1,) + (1,) * (len(dims) - dim - 1))

    loudness = one(*shards[0])
    for cut in shards[1:]:
        loudness = loudness * one(*cut)
    return loudness


def noise(own_key, dims, scale, most, split=(), held_as=jnp.bfloat16):
    entries = jax.random.normal(own_key, dims, jnp.float32) * scale
    if len(split) > 0:
        entries = block_levels(own_key, dims, split, -0.22, 0.18) * entries
    return jnp.clip(entries, min=-most, max=most).astype(held_as)


def setup_inputs(seed: int = 0) -> dict:
    keys = jax.random.split(jax.random.key(seed), 8)
    tokens_home = draw_tokens_home(jax.random.fold_in(keys[7], 71), 0)
    q_weight = draw_q_weight(jax.random.fold_in(keys[7], 71), 0)
    kv_weight = draw_kv_weight(jax.random.fold_in(keys[7], 71), 0)
    pair_tokens = draw_pair_tokens(jax.random.fold_in(keys[7], 71), 0)
    pair_target = draw_pair_target(jax.random.fold_in(keys[7], 71), 0)
    margins = jnp.clip(jax.random.uniform(keys[5], (PAIRS_ALL,), jnp.float32, -20.0, 20.0), -20.0, 20.0)
    grad_attended = noise(keys[6], (N_DP * RECV, HEADS * HEAD), 8.0, 48.0, ((0, 32), (1, 16)))
    return dict(tokens_home=tokens_home, q_weight=q_weight, kv_weight=kv_weight, pair_tokens=pair_tokens, pair_target=pair_target, margins=margins, grad_attended=grad_attended)


BETA = 0.1
SOFT_CAP = 50.0
ROPE_BASE = 10000.0
QUERY_SCALE = 1.0 / 12.0


def rotate(values, position, heading):
    half_size = values.shape[-1] // 2
    frequency = jnp.exp(-jnp.log(ROPE_BASE) * jnp.arange(half_size).astype(jnp.float32) / half_size)
    angles = position.astype(jnp.float32)[:, None] * frequency[None, :]
    cosine = jnp.cos(angles)
    sine_part = heading * jnp.sin(angles)
    leading = values[..., :half_size]
    trailing = values[..., half_size:]
    return jnp.concatenate([leading * cosine - trailing * sine_part, trailing * cosine + leading * sine_part], axis=-1)


def reference(tokens_home, q_weight, kv_weight, pair_tokens, pair_target, margins, grad_attended):
    replicas = pair_target.shape[0] // SPREAD
    count_heads = q_weight.shape[1] // HEAD
    slot_ids = jnp.arange(SPREAD, dtype=jnp.int32)
    home_ids = jnp.arange(replicas, dtype=jnp.int32)
    tokens = pair_tokens.reshape(replicas, SPREAD, 2)
    target = pair_target.reshape(replicas, SPREAD)
    offsets = jnp.mod(target - home_ids[:, None], replicas)
    pair_sizes = tokens[:, :, 0] + tokens[:, :, 1]
    home_start = jnp.cumsum(pair_sizes, axis=1) - pair_sizes
    hit_table = (offsets[:, None, :] == slot_ids[None, :, None]).astype(jnp.int32)
    pair_of = jnp.sum(hit_table * slot_ids[None, None, :], axis=2)
    source = jnp.mod(home_ids[:, None] - slot_ids[None, :], replicas)
    arrive_pair = pair_of[source, slot_ids[None, :]]
    arrive_global = source * SPREAD + arrive_pair
    chosen_in = pair_tokens[arrive_global, 0]
    sizes_in = chosen_in + pair_tokens[arrive_global, 1]
    starts_in = jnp.cumsum(sizes_in, axis=1) - sizes_in
    row_ids = jnp.arange(RECV, dtype=jnp.int32)
    slot_of = jnp.sum((row_ids[None, :, None] >= starts_in[:, None, :]).astype(jnp.int32), axis=2) - 1
    start_row = jnp.take_along_axis(starts_in, slot_of, axis=1)
    chosen_row = jnp.take_along_axis(chosen_in, slot_of, axis=1)
    within_pair = row_ids[None, :] - start_row
    rejected_row = (within_pair >= chosen_row).astype(jnp.int32)
    position = within_pair - rejected_row * chosen_row
    segment = 2 * slot_of + rejected_row
    source_row = jnp.take_along_axis(source, slot_of, axis=1)
    anchor_row = jnp.take_along_axis(home_start[source, arrive_pair], slot_of, axis=1)
    src_rows = source_row * HOME + anchor_row + within_pair
    moved_all = tokens_home[src_rows.reshape(-1)].reshape(replicas, RECV, D)
    margin_row = jnp.take_along_axis(margins[arrive_global], slot_of, axis=1)
    coef_row = BETA * jax.nn.sigmoid(-BETA * margin_row) * (2 * rejected_row - 1).astype(jnp.float32)

    wq_heads = q_weight.reshape(D, count_heads, HEAD).transpose(1, 0, 2)
    wkv_heads = kv_weight.reshape(D, count_heads, HEAD).transpose(1, 0, 2)
    right_side = jnp.concatenate([wq_heads, wkv_heads], axis=2).astype(jnp.float32)

    def replica_pass(replica_items):
        moved_rows, seg_rows, pos_rows, coef_rows, grad_rows = replica_items
        query_raw = jnp.dot(moved_rows, q_weight, preferred_element_type=jnp.float32)
        query_raw = query_raw.reshape(RECV, count_heads, HEAD).transpose(1, 0, 2)
        kv_raw = jnp.dot(moved_rows, kv_weight, preferred_element_type=jnp.float32)
        kv_raw = kv_raw.reshape(RECV, count_heads, HEAD).transpose(1, 0, 2)
        queries = (QUERY_SCALE * rotate(query_raw, pos_rows, 1.0)).astype(jnp.bfloat16)
        key_groups = rotate(kv_raw[0::2], pos_rows, 1.0).astype(jnp.bfloat16)
        value_groups = kv_raw[1::2].astype(jnp.bfloat16)
        key_heads = jnp.repeat(key_groups, 2, axis=0)
        value_heads = jnp.repeat(value_groups, 2, axis=0)
        scores = jnp.einsum("hqd,hkd->hqk", queries.astype(jnp.float32), key_heads.astype(jnp.float32))
        capped = SOFT_CAP * jnp.tanh(scores / SOFT_CAP)
        allowed = (seg_rows[:, None] == seg_rows[None, :]) & (pos_rows[None, :] <= pos_rows[:, None])
        exponent = jnp.where(allowed[None, :, :], jnp.exp(capped), 0.0)
        weights = exponent / jnp.sum(exponent, axis=2, keepdims=True)
        prob_heads = weights.astype(jnp.bfloat16)
        attended = jnp.einsum("hqk,hkd->hqd", prob_heads.astype(jnp.float32), value_heads.astype(jnp.float32)).astype(jnp.bfloat16)
        upstream = (coef_rows[:, None] * grad_rows.astype(jnp.float32)).astype(jnp.bfloat16)
        upstream = upstream.reshape(RECV, count_heads, HEAD).transpose(1, 0, 2)
        dprobs = jnp.einsum("hqd,hkd->hqk", upstream.astype(jnp.float32), value_heads.astype(jnp.float32))
        delta_row = jnp.sum(weights * dprobs, axis=2, keepdims=True)
        dscores = (weights * (dprobs - delta_row) * (1.0 - jnp.square(capped / SOFT_CAP))).astype(jnp.bfloat16)
        dquery = jnp.einsum("hqk,hkd->hqd", dscores.astype(jnp.float32), key_heads.astype(jnp.float32))
        dquery = (QUERY_SCALE * rotate(dquery, pos_rows, -1.0)).astype(jnp.bfloat16)
        dkey_heads = rotate(jnp.einsum("hqk,hqd->hkd", dscores.astype(jnp.float32), queries.astype(jnp.float32)), pos_rows, -1.0)
        dvalue_heads = jnp.einsum("hqk,hqd->hkd", prob_heads.astype(jnp.float32), upstream.astype(jnp.float32))
        dkey = (dkey_heads[0::2] + dkey_heads[1::2]).astype(jnp.bfloat16)
        dvalue = (dvalue_heads[0::2] + dvalue_heads[1::2]).astype(jnp.bfloat16)
        own_grad = jnp.stack([dkey, dvalue], axis=1).reshape(count_heads, RECV, HEAD)
        left_side = jnp.concatenate([dquery, own_grad], axis=2).astype(jnp.float32)
        head_terms = jnp.einsum("hrc,hdc->hrd", left_side, right_side).astype(jnp.bfloat16)
        dmoved = jnp.sum(head_terms.astype(jnp.float32), axis=0).astype(jnp.bfloat16)
        return attended.transpose(1, 0, 2).reshape(RECV, count_heads * HEAD), dmoved

    grad_all = grad_attended.reshape(replicas, RECV, count_heads * HEAD)
    attended_all, dmoved_all = lax.map(replica_pass, (moved_all, segment, position, coef_row, grad_all))

    places = jnp.arange(HOME, dtype=jnp.int32)
    pair_at = jnp.sum((places[None, :, None] >= home_start[:, None, :]).astype(jnp.int32), axis=2) - 1
    home_live = places[None, :] < jnp.sum(pair_sizes, axis=1)[:, None]
    within_home = places[None, :] - jnp.take_along_axis(home_start, pair_at, axis=1)
    offset_home = jnp.take_along_axis(offsets, pair_at, axis=1)
    dest_replica = jnp.mod(home_ids[:, None] + offset_home, replicas)
    dest_row = starts_in[dest_replica, offset_home] + within_home
    flat_index = jnp.where(home_live, dest_replica * RECV + dest_row, 0)
    picked = dmoved_all.reshape(replicas * RECV, D)[flat_index.reshape(-1)].reshape(replicas, HOME, D)
    grad_home = jnp.where(home_live[:, :, None], picked, jnp.zeros_like(picked)).astype(jnp.bfloat16)
    return attended_all.reshape(replicas * RECV, count_heads * HEAD), grad_home.reshape(replicas * HOME, D)
```

```python
import functools

import jax
import jax.numpy as jnp
import numpy as np
from jax import lax
from jax.experimental import pallas as pl
from jax.experimental.pallas import tpu as pltpu
from jax.sharding import PartitionSpec as P

SPREAD = 4
RECV = 512
CAP = 384
HOME = 1536
TAIL = RECV - CAP
HEAD = 128
HALF = 64
WINDOW = 512

BETA = 0.1
SOFT_CAP = 50.0
ROPE_BASE = 10000.0
QUERY_SCALE = 1.0 / 12.0

F32 = jnp.float32
BF16 = jnp.bfloat16

VMEM = pl.BlockSpec(memory_space=pltpu.VMEM)
SMEM = pl.BlockSpec(memory_space=pltpu.SMEM)
NN = (((1,), (0,)), ((), ()))
NT = (((1,), (1,)), ((), ()))
TN = (((0,), (0,)), ((), ()))


def dot(a, b, dims):
    return lax.dot_general(a, b, dims, preferred_element_type=F32)


def call(kernel, outs, in_specs, args, flops, scratch=(), limit=24):
    moved = sum(int(np.prod(o.shape)) * o.dtype.itemsize for o in outs)
    moved += sum(int(np.prod(a.shape)) * a.dtype.itemsize for a in args)
    return pl.pallas_call(
        kernel,
        out_shape=outs,
        in_specs=in_specs,
        out_specs=[VMEM] * len(outs),
        scratch_shapes=list(scratch),
        compiler_params=pltpu.CompilerParams(vmem_limit_bytes=limit << 20),
        cost_estimate=pl.CostEstimate(flops=flops, bytes_accessed=moved, transcendentals=0),
    )(*args)


def sds(shape, dtype):
    return jax.ShapeDtypeStruct(shape, dtype)


def pair_at(tokens, target, home, replica):
    start, running = jnp.int32(0), jnp.int32(0)
    chosen, rejected, index = jnp.int32(0), jnp.int32(0), jnp.int32(0)
    for p in range(SPREAD):
        i = home * SPREAD + p
        hit = target[i] == replica
        c, r = tokens[i, 0], tokens[i, 1]
        start = jnp.where(hit, running, start)
        chosen = jnp.where(hit, c, chosen)
        rejected = jnp.where(hit, r, rejected)
        index = jnp.where(hit, i, index)
        running = running + c + r
    return start, chosen, rejected, index


def around(index, count):
    return lax.rem(index + count, count)


def outgoing(tokens, target, replicas, replica, offset):
    there = around(replica + offset, replicas)
    start, chosen, rejected, _ = pair_at(tokens, target, replica, there)
    place = jnp.int32(0)
    for nearer in range(offset):
        _, c, r, _ = pair_at(tokens, target, around(there - nearer, replicas), there)
        place = place + c + r
    return start, chosen + rejected, place


def window_of(start):
    first = jnp.minimum((start // 16) * 16, HOME - WINDOW)
    return pl.multiple_of(first, 16)


def pack_kernel(replicas, offsets, tokens, target, home, *outs):
    replica = lax.axis_index("dp")
    for offset, out in zip(offsets, outs):
        start, size, place = outgoing(tokens, target, replicas, replica, offset)
        first = window_of(start)
        skip = RECV - out.shape[1]
        column = lax.broadcasted_iota(jnp.int32, (1, out.shape[1]), 1) + skip
        live = (column >= place) & (column < place + size)
        source = jnp.where(live, column - place + start - first, -1)
        row = lax.broadcasted_iota(jnp.int32, (WINDOW, out.shape[1]), 0)
        pick = (row == source).astype(F32).astype(BF16)
        rows = home[pl.ds(first, WINDOW), :]
        out[...] = dot(rows, pick, TN).astype(BF16)


def weights_kernel(q, kv, own, away):
    core = lax.rem(lax.axis_index("mp"), 2)
    for block in range(q.shape[0]):
        own[block, :, :HEAD] = q[block, core]
        own[block, :, HEAD:] = kv[block, core]
        away[block, :, :HEAD] = q[block, 1 - core]
        away[block, :, HEAD:] = kv[block, 1 - core]


def tables_kernel(replicas, tokens, target, margins, frequency, grad, cosine, sine, begin, upstream):
    replica = lax.axis_index("dp")
    row = lax.broadcasted_iota(jnp.int32, (1, RECV), 1)
    first = jnp.zeros((1, RECV), jnp.int32)
    margin = jnp.zeros((1, RECV), F32)
    sign = jnp.zeros((1, RECV), F32)
    place = jnp.int32(0)
    for offset in range(SPREAD):
        home = around(replica - offset, replicas)
        _, chosen, rejected, index = pair_at(tokens, target, home, replica)
        first = jnp.where(row >= place, place, first)
        margin = jnp.where(row >= place, margins[index], margin)
        sign = jnp.where(row >= place, -1.0, sign)
        first = jnp.where(row >= place + chosen, place + chosen, first)
        sign = jnp.where(row >= place + chosen, 1.0, sign)
        place = place + chosen + rejected
    begin[...] = jnp.broadcast_to(first, begin.shape)
    coef = BETA * sign / (1.0 + jnp.exp(BETA * margin))
    upstream[...] = (grad[...].astype(F32).T * coef).astype(BF16)
    angle = (row - first).astype(F32) * frequency[:, :1]
    cosine[...] = jnp.cos(angle)
    sine[...] = jnp.sin(angle)


def block_index(relative):
    place = lax.axis_index("mp")
    x, y = place // 4, lax.rem(place // 2, 2)
    near, far = x + 1 - 2 * lax.rem(x, 2), 3 - x
    across = far + 1 - 2 * lax.rem(far, 2)
    return (x, near, far, across)[relative % 4] * 2 + (y if relative < 4 else 1 - y)


def project_kernel(own, away, *refs):
    pieces, (keep, send) = refs[:-2], refs[-2:]
    mine = jnp.zeros((2 * HEAD, RECV), F32)
    other = jnp.zeros((2 * HEAD, RECV), F32)
    for relative, piece in enumerate(pieces):
        block = block_index(relative)
        mine = mine + dot(own[block], piece[...], TN)
        other = other + dot(away[block], piece[...], TN)
    keep[: 2 * HEAD] = mine
    keep[2 * HEAD :] = other[HEAD:]
    send[: 2 * HEAD] = other
    send[2 * HEAD :] = mine[HEAD:]


def turn(value, cosine, sine):
    low, high = value[:HALF], value[HALF:]
    return jnp.concatenate([low * cosine - high * sine, high * cosine + low * sine], axis=0)


def attention_kernel(kept, got, cosine, sine, begin, upstream, attended, send, held):
    first_core = lax.rem(lax.axis_index("mp"), 2) == 0
    cos, sin = cosine[...], sine[...]
    total = kept[...] + got[...]
    own, other = total[HEAD : 2 * HEAD], total[2 * HEAD :]
    query = (QUERY_SCALE * turn(total[:HEAD], cos, sin)).astype(BF16)
    key = turn(jnp.where(first_core, own, other), cos, sin).astype(BF16)
    value = jnp.where(first_core, other, own).astype(BF16)
    scores = dot(key, query, TN)
    bent = jnp.tanh(scores / SOFT_CAP)
    key_row = lax.broadcasted_iota(jnp.int32, (RECV, RECV), 0)
    query_row = lax.broadcasted_iota(jnp.int32, (RECV, RECV), 1)
    allowed = (key_row <= query_row) & (key_row >= begin[:1, :])
    exponent = jnp.where(allowed, jnp.exp(SOFT_CAP * bent), 0.0)
    weights = exponent * (1.0 / jnp.sum(exponent, axis=0, keepdims=True))
    probs = weights.astype(BF16)
    attended[...] = dot(value, probs, NN).T.astype(BF16)
    up = upstream[...]
    dprobs = dot(value, up, TN)
    delta = jnp.sum(weights * dprobs, axis=0, keepdims=True)
    dscores = (weights * (dprobs - delta) * (1.0 - bent * bent)).astype(BF16)
    dquery = QUERY_SCALE * turn(dot(key, dscores, NN), cos, -sin)
    dkey = turn(dot(query, dscores, NT), cos, -sin)
    dvalue = dot(up, probs, NT)
    down, dother = jnp.where(first_core, dkey, dvalue), jnp.where(first_core, dvalue, dkey)
    send[:HEAD] = dquery.astype(BF16)
    send[HEAD : 2 * HEAD] = down.astype(BF16)
    send[2 * HEAD :] = dother.astype(BF16)
    held[:HEAD] = down
    held[HEAD:] = dother


def spread_kernel(own, away, sent, held, got, *outs):
    down = (held[:HEAD] + got[2 * HEAD :].astype(F32)).astype(BF16)
    dother = (held[HEAD:] + got[HEAD : 2 * HEAD].astype(F32)).astype(BF16)
    mine = jnp.concatenate([sent[:HEAD], down], axis=0)
    other = jnp.concatenate([got[:HEAD], dother], axis=0)
    for relative, out in enumerate(outs):
        block = block_index(relative)
        out[...] = (dot(own[block], mine, NN) + dot(away[block], other, NN)).astype(BF16)


def unpack_kernel(replicas, tokens, target, *refs):
    pieces, (home, total) = refs[:-2], refs[-2:]
    replica = lax.axis_index("dp")
    total[...] = jnp.zeros_like(total)
    for offset, piece in enumerate(pieces):
        start, size, place = outgoing(tokens, target, replicas, replica, offset)
        first = window_of(start)
        skip = RECV - piece.shape[1]
        row = lax.broadcasted_iota(jnp.int32, (WINDOW, piece.shape[1]), 0)
        column = lax.broadcasted_iota(jnp.int32, (1, piece.shape[1]), 1) + skip
        live = (column >= place) & (column < place + size)
        source = jnp.where(live, column - place + start - first, -1)
        pick = (row == source).astype(F32).astype(BF16)
        total[pl.ds(first, WINDOW), :] += dot(pick, piece[...], NT)
    home[...] = total[...].astype(BF16)


def along(value, steps):
    count = lax.axis_size("dp")
    return lax.ppermute(value, "dp", [(s, (s + steps) % count) for s in range(count)])


def swap(value, change):
    count = lax.axis_size("mp")
    pairs = []
    for source in range(count):
        x, y, core = source // 4, source // 2 % 2, source % 2
        x, y, core = change(x, y, core)
        pairs.append((source, x * 4 + y * 2 + core))
    return lax.ppermute(value, "mp", pairs)


def to_core(value):
    return swap(value, lambda x, y, core: (x, y, 1 - core))


def to_y(value):
    return swap(value, lambda x, y, core: (x, 1 - y, core))


def to_near(value):
    return swap(value, lambda x, y, core: (x ^ 1, y, core))


def to_far(value):
    return swap(value, lambda x, y, core: (3 - x, y, core))


def body(tokens_home, q_weight, kv_weight, pair_tokens, pair_target, margins, grad_attended):
    replicas = lax.axis_size("dp")
    blocks = lax.axis_size("mp") // 2
    width = tokens_home.shape[1]
    table = (pair_tokens, pair_target)

    def pack(offsets):
        outs = [sds((width, CAP if o == SPREAD - 1 else RECV), BF16) for o in offsets]
        return call(
            functools.partial(pack_kernel, replicas, offsets),
            outs,
            [SMEM, SMEM, VMEM],
            (*table, tokens_home),
            2 * len(offsets) * width * WINDOW * RECV,
        )

    (third,) = pack((3,))
    bucket = along(third, 1)
    second, first, zeroth = pack((2, 1, 0))
    own_w, away_w = call(
        weights_kernel,
        [sds((blocks, width, 2 * HEAD), BF16)] * 2,
        [VMEM, VMEM],
        (q_weight.reshape(blocks, 2, width, HEAD), kv_weight.reshape(blocks, 2, width, HEAD)),
        1000,
    )
    other_w = to_core(away_w)
    frequency = np.exp(-np.log(ROPE_BASE) * np.arange(HALF) / HALF).astype(np.float32)
    frequency = jnp.asarray(np.broadcast_to(frequency[:, None], (HALF, HEAD)))
    cosine, sine, begin, upstream = call(
        functools.partial(tables_kernel, replicas),
        [sds((HALF, RECV), F32), sds((HALF, RECV), F32), sds((8, RECV), jnp.int32), sds((HEAD, RECV), BF16)],
        [SMEM, SMEM, SMEM, VMEM, VMEM],
        (*table, margins, frequency, grad_attended),
        1000,
    )
    bucket = jnp.pad(bucket, ((0, 0), (TAIL, 0))) + second
    bucket = along(bucket, 1) + first
    moved = along(bucket, 1) + zeroth

    other_y = to_y(moved)
    near = to_near(moved)
    far = to_far(moved)
    across = to_far(near)
    far_y = to_far(other_y)
    near_y = to_near(other_y)
    across_y = to_near(far_y)
    pieces = (moved, near, far, across, other_y, near_y, far_y, across_y)
    keep, send = call(
        project_kernel,
        [sds((3 * HEAD, RECV), F32)] * 2,
        [VMEM] * 10,
        (own_w, other_w, *pieces),
        2 * blocks * width * 4 * HEAD * RECV,
    )
    got = to_core(send)
    attended, send, held = call(
        attention_kernel,
        [sds((RECV, HEAD), BF16), sds((3 * HEAD, RECV), BF16), sds((2 * HEAD, RECV), F32)],
        [VMEM] * 6,
        (keep, got, cosine, sine, begin, upstream),
        14 * HEAD * RECV * RECV,
    )
    got = to_core(send)
    parts = call(
        spread_kernel,
        [sds((width, RECV), BF16)] * 8,
        [VMEM] * 5,
        (own_w, other_w, send, held, got),
        2 * blocks * width * 4 * HEAD * RECV,
    )
    mine, near, far, across, mine_y, near_y, far_y, across_y = parts

    def plus(*terms):
        return sum(t.astype(F32) for t in terms).astype(BF16)

    forward_y = plus(far_y, to_near(across_y))
    forward = plus(near, to_far(across))
    here_y = plus(mine_y, to_near(near_y), to_far(forward_y))
    here = plus(mine, to_far(far), to_near(forward), to_y(here_y))

    back1 = along(here, -1)
    back2 = along(back1, -1)
    back3 = along(back2[:, TAIL:], -1)
    (grad_home,) = call(
        functools.partial(unpack_kernel, replicas),
        [sds((HOME, width), BF16)],
        [SMEM, SMEM] + [VMEM] * 4,
        (*table, here, back1, back2, back3),
        2 * SPREAD * width * WINDOW * RECV,
        scratch=[pltpu.VMEM((HOME, width), F32)],
    )
    return (attended, grad_home)


def solution(mesh):
    return jax.shard_map(
        body,
        mesh=mesh,
        in_specs=(P("dp", "mp"), P(None, "mp"), P(None, "mp"), P(), P(), P(), P("dp", "mp")),
        out_specs=(P("dp", "mp"), P("dp", "mp")),
        check_vma=False,
    )
```

```python
import functools

import jax
import jax.numpy as jnp
import numpy as np
from jax import lax
from jax.experimental import pallas as pl
from jax.experimental.pallas import tpu as pltpu
from jax.sharding import PartitionSpec as P

SPREAD = 4
RECV = 512
CAP = 384
HOME = 1536
TAIL = RECV - CAP
HEAD = 128
HALF = 64
WINDOW = 512

BETA = 0.1
SOFT_CAP = 50.0
ROPE_BASE = 10000.0
QUERY_SCALE = 1.0 / 12.0

F32 = jnp.float32
BF16 = jnp.bfloat16

VMEM = pl.BlockSpec(memory_space=pltpu.VMEM)
SMEM = pl.BlockSpec(memory_space=pltpu.SMEM)
NN = (((1,), (0,)), ((), ()))
NT = (((1,), (1,)), ((), ()))
TN = (((0,), (0,)), ((), ()))


def dot(a, b, dims):
    return lax.dot_general(a, b, dims, preferred_element_type=F32)


def call(kernel, outs, in_specs, args, flops, scratch=(), limit=24):
    moved = sum(int(np.prod(o.shape)) * o.dtype.itemsize for o in outs)
    moved += sum(int(np.prod(a.shape)) * a.dtype.itemsize for a in args)
    return pl.pallas_call(
        kernel,
        out_shape=outs,
        in_specs=in_specs,
        out_specs=[VMEM] * len(outs),
        scratch_shapes=list(scratch),
        compiler_params=pltpu.CompilerParams(vmem_limit_bytes=limit << 20),
        cost_estimate=pl.CostEstimate(flops=flops, bytes_accessed=moved, transcendentals=0),
    )(*args)


def sds(shape, dtype):
    return jax.ShapeDtypeStruct(shape, dtype)


def pair_at(tokens, target, home, replica):
    start, running = jnp.int32(0), jnp.int32(0)
    chosen, rejected, index = jnp.int32(0), jnp.int32(0), jnp.int32(0)
    for p in range(SPREAD):
        i = home * SPREAD + p
        hit = target[i] == replica
        c, r = tokens[0, i], tokens[1, i]
        start = jnp.where(hit, running, start)
        chosen = jnp.where(hit, c, chosen)
        rejected = jnp.where(hit, r, rejected)
        index = jnp.where(hit, i, index)
        running = running + c + r
    return start, chosen, rejected, index


def around(index, count):
    return lax.rem(index + count, count)


def outgoing(tokens, target, replicas, replica, offset):
    there = around(replica + offset, replicas)
    start, chosen, rejected, _ = pair_at(tokens, target, replica, there)
    place = jnp.int32(0)
    for nearer in range(offset):
        _, c, r, _ = pair_at(tokens, target, around(there - nearer, replicas), there)
        place = place + c + r
    return start, chosen + rejected, place


def window_of(start):
    first = jnp.minimum((start // 128) * 128, HOME - WINDOW)
    return pl.multiple_of(first, 128)


def pack_one(replicas, offset, tokens, target, home, out, wait=None):
    replica = lax.axis_index("dp")
    start, size, place = outgoing(tokens, target, replicas, replica, offset)
    first = window_of(start)
    columns = out.shape[1]
    column = lax.broadcasted_iota(jnp.int32, (1, columns), 1) + RECV - columns
    live = (column >= place) & (column < place + size)
    source = jnp.where(live, column - place + start - first, -1)
    row = lax.broadcasted_iota(jnp.int32, (WINDOW, columns), 0)
    pick = jnp.where(row == source, 1.0, 0.0).astype(BF16)
    if wait is not None:
        wait()
    out[...] = dot(home[:, pl.ds(first, WINDOW)], pick, NN).astype(BF16)


def pack_first_kernel(replicas, tokens, target, home, out, tokens_in, target_in, home_in, sems):
    copies = [
        pltpu.make_async_copy(source, place, sems.at[i])
        for i, (source, place) in enumerate(
            ((tokens, tokens_in), (target, target_in), (home, home_in))
        )
    ]
    for copy in copies:
        copy.start()
    copies[0].wait()
    copies[1].wait()
    pack_one(replicas, SPREAD - 1, tokens_in, target_in, home_in, out, copies[2].wait)


def pack_kernel(replicas, offsets, tokens, target, home, *outs):
    for offset, out in zip(offsets, outs):
        pack_one(replicas, offset, tokens, target, home, out)


def weights_kernel(q, kv, own, away):
    core = lax.rem(lax.axis_index("mp"), 2)
    for block in range(q.shape[0]):
        own[block, :, :HEAD] = q[block, core]
        own[block, :, HEAD:] = kv[block, core]
        away[block, :, :HEAD] = q[block, 1 - core]
        away[block, :, HEAD:] = kv[block, 1 - core]


def turned_kernel(own, away, out):
    for block in range(own.shape[0]):
        out[block, : 2 * HEAD] = own[block].astype(F32).T.astype(BF16)
        out[block, 2 * HEAD :] = away[block].astype(F32).T.astype(BF16)


def tables_kernel(replicas, tokens, target, margins, frequency, grad, cosine, sine, begin, upstream):
    replica = lax.axis_index("dp")
    row = lax.broadcasted_iota(jnp.int32, (1, RECV), 1)
    first = jnp.zeros((1, RECV), jnp.int32)
    margin = jnp.zeros((1, RECV), F32)
    sign = jnp.zeros((1, RECV), F32)
    place = jnp.int32(0)
    for offset in range(SPREAD):
        home = around(replica - offset, replicas)
        _, chosen, rejected, index = pair_at(tokens, target, home, replica)
        first = jnp.where(row >= place, place, first)
        margin = jnp.where(row >= place, margins[index], margin)
        sign = jnp.where(row >= place, -1.0, sign)
        first = jnp.where(row >= place + chosen, place + chosen, first)
        sign = jnp.where(row >= place + chosen, 1.0, sign)
        place = place + chosen + rejected
    begin[...] = jnp.broadcast_to(first, begin.shape)
    coef = BETA * sign / (1.0 + jnp.exp(BETA * margin))
    upstream[...] = (grad[...].astype(F32).T * coef).astype(BF16)
    angle = (row - first).astype(F32) * frequency[:, :1]
    cosine[...] = jnp.cos(angle)
    sine[...] = jnp.sin(angle)


def block_index(relative):
    place = lax.axis_index("mp")
    x, y = place // 4, lax.rem(place // 2, 2)
    near, far = x + 1 - 2 * lax.rem(x, 2), 3 - x
    across = far + 1 - 2 * lax.rem(far, 2)
    return (x, near, far, across)[relative % 4] * 2 + (y if relative < 4 else 1 - y)


def partial_products(turned, pieces, numbers):
    total = None
    for relative, piece in zip(numbers, pieces):
        term = dot(turned[block_index(relative)], piece[...], NN)
        total = term if total is None else total + term
    return total


def project_kernel(numbers, turned, *refs):
    pieces, out = refs[:-1], refs[-1]
    out[...] = partial_products(turned, pieces, numbers)


def project_last_kernel(numbers, turned, before, *refs):
    pieces, (keep, send) = refs[:-2], refs[-2:]
    total = before[...] + partial_products(turned, pieces, numbers)
    keep[: 2 * HEAD] = total[: 2 * HEAD]
    keep[2 * HEAD :] = total[3 * HEAD :]
    send[: 2 * HEAD] = total[2 * HEAD :].astype(BF16)
    send[2 * HEAD :] = total[HEAD : 2 * HEAD].astype(BF16)


def turn(value, cosine, sine):
    low, high = value[:HALF], value[HALF:]
    return jnp.concatenate([low * cosine - high * sine, high * cosine + low * sine], axis=0)


def attention_kernel(kept, got, cosine, sine, begin, upstream, attended, send, held):
    core = lax.rem(lax.axis_index("mp"), 2)
    first_core = core == 0
    cos, sin = cosine[...], sine[...]
    total = kept[...] + got[1 - core].astype(F32)
    own, other = total[HEAD : 2 * HEAD], total[2 * HEAD :]
    query = (QUERY_SCALE * turn(total[:HEAD], cos, sin)).astype(BF16)
    key = turn(jnp.where(first_core, own, other), cos, sin).astype(BF16)
    value = jnp.where(first_core, other, own).astype(BF16)
    scores = dot(key, query, TN)
    bent = jnp.tanh(scores / SOFT_CAP)
    key_row = lax.broadcasted_iota(jnp.int32, (RECV, RECV), 0)
    query_row = lax.broadcasted_iota(jnp.int32, (RECV, RECV), 1)
    allowed = (key_row <= query_row) & (key_row >= begin[:1, :])
    exponent = jnp.where(allowed, jnp.exp(SOFT_CAP * bent), 0.0)
    weights = exponent * (1.0 / jnp.sum(exponent, axis=0, keepdims=True))
    probs = weights.astype(BF16)
    attended[...] = dot(value, probs, NN).T.astype(BF16)
    up = upstream[...]
    dprobs = dot(value, up, TN)
    delta = jnp.sum(weights * dprobs, axis=0, keepdims=True)
    dscores = (weights * (dprobs - delta) * (1.0 - bent * bent)).astype(BF16)
    dquery = QUERY_SCALE * turn(dot(key, dscores, NN), cos, -sin)
    dkey = turn(dot(query, dscores, NT), cos, -sin)
    dvalue = dot(up, probs, NT)
    down, dother = jnp.where(first_core, dkey, dvalue), jnp.where(first_core, dvalue, dkey)
    send[:HEAD] = dquery.astype(BF16)
    send[HEAD : 2 * HEAD] = down.astype(BF16)
    send[2 * HEAD :] = dother.astype(BF16)
    held[:HEAD] = down
    held[HEAD:] = dother


def gradients(sent, held, both):
    got = both.at[1 - lax.rem(lax.axis_index("mp"), 2)]
    down = (held[:HEAD] + got[2 * HEAD :].astype(F32)).astype(BF16)
    dother = (held[HEAD:] + got[HEAD : 2 * HEAD].astype(F32)).astype(BF16)
    mine = jnp.concatenate([sent[:HEAD], down], axis=0)
    other = jnp.concatenate([got[:HEAD], dother], axis=0)
    return mine, other


def spread_kernel(numbers, own, away, sent, held, got, *outs):
    mine, other = gradients(sent, held, got)
    for relative, out in zip(numbers, outs):
        block = block_index(relative)
        out[...] = (dot(own[block], mine, NN) + dot(away[block], other, NN)).astype(BF16)


def unpack_one(replicas, offset, tokens, target, piece):
    replica = lax.axis_index("dp")
    start, size, place = outgoing(tokens, target, replicas, replica, offset)
    first = window_of(start)
    columns = piece.shape[1]
    column = lax.broadcasted_iota(jnp.int32, (columns, 1), 0) + RECV - columns
    live = (column >= place) & (column < place + size)
    dest = jnp.where(live, column - place + start - first, -1)
    spot = lax.broadcasted_iota(jnp.int32, (columns, WINDOW), 1)
    pick = jnp.where(spot == dest, 1.0, 0.0).astype(BF16)
    return first, dot(piece[...], pick, NN)


def unpack_kernel(replicas, tokens, target, *refs):
    pieces, (home, last) = refs[:-2], refs[-2:]
    home[...] = jnp.zeros_like(home)
    for offset, piece in enumerate(pieces):
        first, back = unpack_one(replicas, offset, tokens, target, piece)
        window = home[:, pl.ds(first, WINDOW)]
        home[:, pl.ds(first, WINDOW)] = (window.astype(F32) + back).astype(BF16)
    replica = lax.axis_index("dp")
    start, _, _ = outgoing(tokens, target, replicas, replica, SPREAD - 1)
    last[...] = home[:, pl.ds(window_of(start), WINDOW)]


def unpack_last_kernel(replicas, tokens, target, window, piece, home, out, whole, sem):
    first, back = unpack_one(replicas, SPREAD - 1, tokens, target, piece)
    whole[...] = (window[...].astype(F32) + back).astype(BF16)
    copy = pltpu.make_async_copy(whole, out.at[:, pl.ds(first, WINDOW)], sem)
    copy.start()
    copy.wait()


def along(value, steps):
    count = lax.axis_size("dp")
    return lax.ppermute(value, "dp", [(s, (s + steps) % count) for s in range(count)])


def swap(value, change):
    count = lax.axis_size("mp")
    pairs = []
    for source in range(count):
        x, y, core = source // 4, source // 2 % 2, source % 2
        x, y, core = change(x, y, core)
        pairs.append((source, x * 4 + y * 2 + core))
    return lax.ppermute(value, "mp", pairs)


def to_core(value):
    return swap(value, lambda x, y, core: (x, y, 1 - core))


def of_cores(value):
    count = lax.axis_size("mp")
    groups = [[place, place + 1] for place in range(0, count, 2)]
    return lax.all_gather(value, "mp", axis_index_groups=groups)


def to_y(value):
    return swap(value, lambda x, y, core: (x, 1 - y, core))


def to_near(value):
    return swap(value, lambda x, y, core: (x ^ 1, y, core))


def to_far(value):
    return swap(value, lambda x, y, core: (3 - x, y, core))


def plus(*terms):
    return sum(t.astype(F32) for t in terms).astype(BF16)


def body(tokens_home, q_weight, kv_weight, pair_tokens, pair_target, margins, grad_attended):
    replicas = lax.axis_size("dp")
    blocks = lax.axis_size("mp") // 2
    width = tokens_home.shape[1]
    table = (pair_tokens.T, pair_target)
    home = tokens_home.T

    third = pl.pallas_call(
        functools.partial(pack_first_kernel, replicas),
        out_shape=sds((width, CAP), BF16),
        in_specs=[pl.BlockSpec(memory_space=pl.ANY)] * 3,
        out_specs=VMEM,
        scratch_shapes=[
            pltpu.SMEM(table[0].shape, jnp.int32),
            pltpu.SMEM(table[1].shape, jnp.int32),
            pltpu.VMEM(home.shape, BF16),
            pltpu.SemaphoreType.DMA((3,)),
        ],
        compiler_params=pltpu.CompilerParams(vmem_limit_bytes=60 << 20),
        cost_estimate=pl.CostEstimate(
            flops=2 * width * WINDOW * CAP, bytes_accessed=2 * width * HOME, transcendentals=0
        ),
    )(*table, home)
    bucket = along(third, 1)
    (first,) = call(
        functools.partial(pack_kernel, replicas, (1,)),
        [sds((width, RECV), BF16)],
        [SMEM, SMEM, VMEM],
        (*table, home),
        2 * width * WINDOW * RECV,
    )
    first = along(first, 1)
    second, zeroth = call(
        functools.partial(pack_kernel, replicas, (2, 0)),
        [sds((width, RECV), BF16)] * 2,
        [SMEM, SMEM, VMEM],
        (*table, home),
        4 * width * WINDOW * RECV,
    )
    frequency = np.exp(-np.log(ROPE_BASE) * np.arange(HALF) / HALF).astype(np.float32)
    frequency = jnp.asarray(np.broadcast_to(frequency[:, None], (HALF, HEAD)))
    tables = call(
        functools.partial(tables_kernel, replicas),
        [sds((HALF, RECV), F32), sds((HALF, RECV), F32), sds((8, RECV), jnp.int32), sds((HEAD, RECV), BF16)],
        [SMEM, SMEM, SMEM, VMEM, VMEM],
        (*table, margins, frequency, grad_attended),
        1000,
    )
    own_w, away_w = call(
        weights_kernel,
        [sds((blocks, width, 2 * HEAD), BF16)] * 2,
        [VMEM, VMEM],
        (q_weight.reshape(blocks, 2, width, HEAD), kv_weight.reshape(blocks, 2, width, HEAD)),
        1000,
    )
    other_w = to_core(away_w)
    bucket = jnp.pad(bucket, ((0, 0), (TAIL, 0))) + second
    bucket, tables, own_w = lax.optimization_barrier((bucket, tables, own_w))
    (turned,) = call(
        turned_kernel,
        [sds((blocks, 4 * HEAD, width), BF16)],
        [VMEM, VMEM],
        (own_w, other_w),
        1000,
    )
    mine = along(bucket, 2) + first + zeroth

    mine_y = to_y(mine)
    near = to_near(mine)
    far = to_far(mine)
    far_y = to_far(mine_y)
    near_y = to_near(mine_y)
    across = to_far(near)
    across_y = to_near(far_y)
    (before,) = call(
        functools.partial(project_kernel, (0, 1, 4, 6)),
        [sds((4 * HEAD, RECV), F32)],
        [VMEM] * 5,
        (turned, mine, near, mine_y, far_y),
        blocks * width * 4 * HEAD * RECV,
    )
    keep, send = call(
        functools.partial(project_last_kernel, (2, 3, 5, 7)),
        [sds((3 * HEAD, RECV), F32), sds((3 * HEAD, RECV), BF16)],
        [VMEM] * 6,
        (turned, before, far, across, near_y, across_y),
        blocks * width * 4 * HEAD * RECV,
    )
    got = of_cores(send)
    attended, send, held = call(
        attention_kernel,
        [sds((RECV, HEAD), BF16), sds((3 * HEAD, RECV), BF16), sds((2 * HEAD, RECV), F32)],
        [VMEM] * 6,
        (keep, got, *tables),
        14 * HEAD * RECV * RECV,
    )
    got = of_cores(send)

    def spread(numbers):
        return call(
            functools.partial(spread_kernel, numbers),
            [sds((width, RECV), BF16)] * len(numbers),
            [VMEM] * 5,
            (own_w, other_w, send, held, got),
            len(numbers) * width * 8 * HEAD * RECV,
        )

    across_y, far, near_y, across = spread((7, 2, 5, 3))
    mine, near, mine_y, far_y = spread((0, 1, 4, 6))
    forward_y = plus(far_y, to_near(across_y))
    forward = plus(near, to_far(across))
    here_y = plus(mine_y, to_near(near_y), to_far(forward_y))
    here = plus(mine, to_far(far), to_near(forward), to_y(here_y))

    back1 = along(here, -1)
    back2 = along(back1, -1)
    back3 = along(back2[:, TAIL:], -1)
    most, window = call(
        functools.partial(unpack_kernel, replicas),
        [sds((width, HOME), BF16), sds((width, WINDOW), BF16)],
        [SMEM, SMEM, VMEM, VMEM, VMEM],
        (*table, here, back1, back2),
        6 * width * WINDOW * RECV,
    )
    grad_home = pl.pallas_call(
        functools.partial(unpack_last_kernel, replicas),
        out_shape=sds((width, HOME), BF16),
        in_specs=[SMEM, SMEM, VMEM, VMEM, pl.BlockSpec(memory_space=pl.ANY)],
        out_specs=pl.BlockSpec(memory_space=pl.ANY),
        scratch_shapes=[pltpu.VMEM((width, WINDOW), BF16), pltpu.SemaphoreType.DMA],
        input_output_aliases={4: 0},
        compiler_params=pltpu.CompilerParams(vmem_limit_bytes=24 << 20),
        cost_estimate=pl.CostEstimate(
            flops=2 * width * WINDOW * CAP, bytes_accessed=4 * width * WINDOW, transcendentals=0
        ),
    )(*table, window, back3, most)
    return (attended, grad_home.T)


def solution(mesh):
    return jax.shard_map(
        body,
        mesh=mesh,
        in_specs=(P("dp", "mp"), P(None, "mp"), P(None, "mp"), P(), P(), P(), P("dp", "mp")),
        out_specs=(P("dp", "mp"), P("dp", "mp")),
        check_vma=False,
    )
```

```python
import functools

import jax
import jax.numpy as jnp
import numpy as np
from jax import lax
from jax.experimental import pallas as pl
from jax.experimental.pallas import tpu as pltpu
from jax.sharding import PartitionSpec as P

SPREAD = 4
RECV = 512
CAP = 384
HOME = 1536
TAIL = RECV - CAP
HEAD = 128
HALF = 64
WINDOW = 512

BETA = 0.1
SOFT_CAP = 50.0
ROPE_BASE = 10000.0
QUERY_SCALE = 1.0 / 12.0

F32 = jnp.float32
BF16 = jnp.bfloat16

VMEM = pl.BlockSpec(memory_space=pltpu.VMEM)
SMEM = pl.BlockSpec(memory_space=pltpu.SMEM)
NN = (((1,), (0,)), ((), ()))
NT = (((1,), (1,)), ((), ()))
TN = (((0,), (0,)), ((), ()))


def dot(a, b, dims):
    return lax.dot_general(a, b, dims, preferred_element_type=F32)


def call(kernel, outs, in_specs, args, flops, scratch=(), limit=24):
    moved = sum(int(np.prod(o.shape)) * o.dtype.itemsize for o in outs)
    moved += sum(int(np.prod(a.shape)) * a.dtype.itemsize for a in args)
    return pl.pallas_call(
        kernel,
        out_shape=outs,
        in_specs=in_specs,
        out_specs=[VMEM] * len(outs),
        scratch_shapes=list(scratch),
        compiler_params=pltpu.CompilerParams(vmem_limit_bytes=limit << 20),
        cost_estimate=pl.CostEstimate(flops=flops, bytes_accessed=moved, transcendentals=0),
    )(*args)


def sds(shape, dtype):
    return jax.ShapeDtypeStruct(shape, dtype)


def pair_at(tokens, target, home, replica):
    start, running = jnp.int32(0), jnp.int32(0)
    chosen, rejected, index = jnp.int32(0), jnp.int32(0), jnp.int32(0)
    for p in range(SPREAD):
        i = home * SPREAD + p
        hit = target[i] == replica
        c, r = tokens[0, i], tokens[1, i]
        start = jnp.where(hit, running, start)
        chosen = jnp.where(hit, c, chosen)
        rejected = jnp.where(hit, r, rejected)
        index = jnp.where(hit, i, index)
        running = running + c + r
    return start, chosen, rejected, index


def around(index, count):
    return lax.rem(index + count, count)


def outgoing(tokens, target, replicas, replica, offset):
    there = around(replica + offset, replicas)
    start, chosen, rejected, _ = pair_at(tokens, target, replica, there)
    place = jnp.int32(0)
    for nearer in range(offset):
        _, c, r, _ = pair_at(tokens, target, around(there - nearer, replicas), there)
        place = place + c + r
    return start, chosen + rejected, place


def window_of(start):
    first = jnp.minimum((start // 128) * 128, HOME - WINDOW)
    return pl.multiple_of(first, 128)


def pack_one(replicas, offset, tokens, target, home, out, wait=None):
    replica = lax.axis_index("dp")
    start, size, place = outgoing(tokens, target, replicas, replica, offset)
    first = window_of(start)
    columns = out.shape[1]
    column = lax.broadcasted_iota(jnp.int32, (1, columns), 1) + RECV - columns
    live = (column >= place) & (column < place + size)
    source = jnp.where(live, column - place + start - first, -1)
    row = lax.broadcasted_iota(jnp.int32, (WINDOW, columns), 0)
    pick = jnp.where(row == source, 1.0, 0.0).astype(BF16)
    if wait is not None:
        wait()
    out[...] = dot(home[:, pl.ds(first, WINDOW)], pick, NN).astype(BF16)


def pack_first_kernel(replicas, tokens, target, home, out, tokens_in, target_in, home_in, sems):
    copies = [
        pltpu.make_async_copy(source, place, sems.at[i])
        for i, (source, place) in enumerate(
            ((tokens, tokens_in), (target, target_in), (home, home_in))
        )
    ]
    for copy in copies:
        copy.start()
    copies[0].wait()
    copies[1].wait()
    pack_one(replicas, SPREAD - 1, tokens_in, target_in, home_in, out, copies[2].wait)


def pack_kernel(replicas, offsets, tokens, target, home, *outs):
    for offset, out in zip(offsets, outs):
        pack_one(replicas, offset, tokens, target, home, out)


def weights_kernel(q, kv, own, away):
    core = lax.rem(lax.axis_index("mp"), 2)
    for block in range(q.shape[0]):
        own[block, :, :HEAD] = q[block, core]
        own[block, :, HEAD:] = kv[block, core]
        away[block, :, :HEAD] = q[block, 1 - core]
        away[block, :, HEAD:] = kv[block, 1 - core]


def turned_kernel(own, away, out):
    for block in range(own.shape[0]):
        out[block, : 2 * HEAD] = own[block].astype(F32).T.astype(BF16)
        out[block, 2 * HEAD :] = away[block].astype(F32).T.astype(BF16)


def tables_kernel(replicas, tokens, target, margins, frequency, grad, cosine, sine, begin, upstream):
    replica = lax.axis_index("dp")
    row = lax.broadcasted_iota(jnp.int32, (1, RECV), 1)
    first = jnp.zeros((1, RECV), jnp.int32)
    margin = jnp.zeros((1, RECV), F32)
    sign = jnp.zeros((1, RECV), F32)
    place = jnp.int32(0)
    for offset in range(SPREAD):
        home = around(replica - offset, replicas)
        _, chosen, rejected, index = pair_at(tokens, target, home, replica)
        first = jnp.where(row >= place, place, first)
        margin = jnp.where(row >= place, margins[index], margin)
        sign = jnp.where(row >= place, -1.0, sign)
        first = jnp.where(row >= place + chosen, place + chosen, first)
        sign = jnp.where(row >= place + chosen, 1.0, sign)
        place = place + chosen + rejected
    begin[...] = jnp.broadcast_to(first, begin.shape)
    coef = BETA * sign / (1.0 + jnp.exp(BETA * margin))
    upstream[...] = (grad[...].astype(F32).T * coef).astype(BF16)
    angle = (row - first).astype(F32) * frequency[:, :1]
    cosine[...] = jnp.cos(angle)
    sine[...] = jnp.sin(angle)


def block_index(relative):
    place = lax.axis_index("mp")
    x, y = place // 4, lax.rem(place // 2, 2)
    near, far = x + 1 - 2 * lax.rem(x, 2), 3 - x
    across = far + 1 - 2 * lax.rem(far, 2)
    return (x, near, far, across)[relative % 4] * 2 + (y if relative < 4 else 1 - y)


def partial_products(turned, pieces, numbers):
    total = None
    for relative, piece in zip(numbers, pieces):
        term = dot(turned[block_index(relative)], piece[...], NN)
        total = term if total is None else total + term
    return total


def project_kernel(numbers, turned, *refs):
    pieces, out = refs[:-1], refs[-1]
    out[...] = partial_products(turned, pieces, numbers)


def project_last_kernel(numbers, turned, before, *refs):
    pieces, (keep, send) = refs[:-2], refs[-2:]
    total = before[...] + partial_products(turned, pieces, numbers)
    keep[: 2 * HEAD] = total[: 2 * HEAD]
    keep[2 * HEAD :] = total[3 * HEAD :]
    send[: 2 * HEAD] = total[2 * HEAD :].astype(BF16)
    send[2 * HEAD :] = total[HEAD : 2 * HEAD].astype(BF16)


def turn(value, cosine, sine):
    low, high = value[:HALF], value[HALF:]
    return jnp.concatenate([low * cosine - high * sine, high * cosine + low * sine], axis=0)


def attention_kernel(kept, got, cosine, sine, begin, upstream, attended, send, held):
    core = lax.rem(lax.axis_index("mp"), 2)
    first_core = core == 0
    cos, sin = cosine[...], sine[...]
    total = kept[...] + got[1 - core].astype(F32)
    own, other = total[HEAD : 2 * HEAD], total[2 * HEAD :]
    query = (QUERY_SCALE * turn(total[:HEAD], cos, sin)).astype(BF16)
    key = turn(jnp.where(first_core, own, other), cos, sin).astype(BF16)
    value = jnp.where(first_core, other, own).astype(BF16)
    scores = dot(key, query, TN)
    bent = jnp.tanh(scores / SOFT_CAP)
    key_row = lax.broadcasted_iota(jnp.int32, (RECV, RECV), 0)
    query_row = lax.broadcasted_iota(jnp.int32, (RECV, RECV), 1)
    allowed = (key_row <= query_row) & (key_row >= begin[:1, :])
    exponent = jnp.where(allowed, jnp.exp(SOFT_CAP * bent), 0.0)
    weights = exponent * (1.0 / jnp.sum(exponent, axis=0, keepdims=True))
    probs = weights.astype(BF16)
    attended[...] = dot(value, probs, NN).T.astype(BF16)
    up = upstream[...]
    dprobs = dot(value, up, TN)
    delta = jnp.sum(weights * dprobs, axis=0, keepdims=True)
    dscores = (weights * (dprobs - delta) * (1.0 - bent * bent)).astype(BF16)
    dquery = QUERY_SCALE * turn(dot(key, dscores, NN), cos, -sin)
    dkey = turn(dot(query, dscores, NT), cos, -sin)
    dvalue = dot(up, probs, NT)
    down, dother = jnp.where(first_core, dkey, dvalue), jnp.where(first_core, dvalue, dkey)
    send[:HEAD] = dquery.astype(BF16)
    send[HEAD : 2 * HEAD] = down.astype(BF16)
    send[2 * HEAD :] = dother.astype(BF16)
    held[:HEAD] = down
    held[HEAD:] = dother


def gradients(sent, held, both):
    got = both.at[1 - lax.rem(lax.axis_index("mp"), 2)]
    down = (held[:HEAD] + got[2 * HEAD :].astype(F32)).astype(BF16)
    dother = (held[HEAD:] + got[HEAD : 2 * HEAD].astype(F32)).astype(BF16)
    mine = jnp.concatenate([sent[:HEAD], down], axis=0)
    other = jnp.concatenate([got[:HEAD], dother], axis=0)
    return mine, other


def spread_kernel(numbers, own, away, sent, held, got, *outs):
    mine, other = gradients(sent, held, got)
    for relative, out in zip(numbers, outs):
        block = block_index(relative)
        out[...] = (dot(own[block], mine, NN) + dot(away[block], other, NN)).astype(BF16)


def unpack_one(replicas, offset, tokens, target, piece):
    replica = lax.axis_index("dp")
    start, size, place = outgoing(tokens, target, replicas, replica, offset)
    first = window_of(start)
    columns = piece.shape[1]
    column = lax.broadcasted_iota(jnp.int32, (columns, 1), 0) + RECV - columns
    live = (column >= place) & (column < place + size)
    dest = jnp.where(live, column - place + start - first, -1)
    spot = lax.broadcasted_iota(jnp.int32, (columns, WINDOW), 1)
    pick = jnp.where(spot == dest, 1.0, 0.0).astype(BF16)
    return first, dot(piece[...], pick, NN)


def unpack_kernel(replicas, tokens, target, *refs):
    pieces, (home, last) = refs[:-2], refs[-2:]
    home[...] = jnp.zeros_like(home)
    for offset, piece in enumerate(pieces):
        first, back = unpack_one(replicas, offset, tokens, target, piece)
        window = home[:, pl.ds(first, WINDOW)]
        home[:, pl.ds(first, WINDOW)] = (window.astype(F32) + back).astype(BF16)
    replica = lax.axis_index("dp")
    start, _, _ = outgoing(tokens, target, replicas, replica, SPREAD - 1)
    last[...] = home[:, pl.ds(window_of(start), WINDOW)]


def unpack_last_kernel(replicas, tokens, target, window, piece, home, out, whole, sem):
    first, back = unpack_one(replicas, SPREAD - 1, tokens, target, piece)
    whole[...] = (window[...].astype(F32) + back).astype(BF16)
    copy = pltpu.make_async_copy(whole, out.at[:, pl.ds(first, WINDOW)], sem)
    copy.start()
    copy.wait()


def along(value, steps):
    count = lax.axis_size("dp")
    return lax.ppermute(value, "dp", [(s, (s + steps) % count) for s in range(count)])


def swap(value, change):
    count = lax.axis_size("mp")
    pairs = []
    for source in range(count):
        x, y, core = source // 4, source // 2 % 2, source % 2
        x, y, core = change(x, y, core)
        pairs.append((source, x * 4 + y * 2 + core))
    return lax.ppermute(value, "mp", pairs)


def to_core(value):
    return swap(value, lambda x, y, core: (x, y, 1 - core))


def of_cores(value):
    count = lax.axis_size("mp")
    groups = [[place, place + 1] for place in range(0, count, 2)]
    return lax.all_gather(value, "mp", axis_index_groups=groups)


def to_y(value):
    return swap(value, lambda x, y, core: (x, 1 - y, core))


def to_near(value):
    return swap(value, lambda x, y, core: (x ^ 1, y, core))


def to_far(value):
    return swap(value, lambda x, y, core: (3 - x, y, core))


def plus(*terms):
    return sum(t.astype(F32) for t in terms).astype(BF16)


def body(tokens_home, q_weight, kv_weight, pair_tokens, pair_target, margins, grad_attended):
    replicas = lax.axis_size("dp")
    blocks = lax.axis_size("mp") // 2
    width = tokens_home.shape[1]
    table = (pair_tokens.T, pair_target)
    home = tokens_home.T

    third = pl.pallas_call(
        functools.partial(pack_first_kernel, replicas),
        out_shape=sds((width, CAP), BF16),
        in_specs=[pl.BlockSpec(memory_space=pl.ANY)] * 3,
        out_specs=VMEM,
        scratch_shapes=[
            pltpu.SMEM(table[0].shape, jnp.int32),
            pltpu.SMEM(table[1].shape, jnp.int32),
            pltpu.VMEM(home.shape, BF16),
            pltpu.SemaphoreType.DMA((3,)),
        ],
        compiler_params=pltpu.CompilerParams(vmem_limit_bytes=60 << 20),
        cost_estimate=pl.CostEstimate(
            flops=2 * width * WINDOW * CAP, bytes_accessed=2 * width * HOME, transcendentals=0
        ),
    )(*table, home)
    bucket = along(third, 1)
    (first,) = call(
        functools.partial(pack_kernel, replicas, (1,)),
        [sds((width, RECV), BF16)],
        [SMEM, SMEM, VMEM],
        (*table, home),
        2 * width * WINDOW * RECV,
    )
    first = along(first, 1)
    second, zeroth = call(
        functools.partial(pack_kernel, replicas, (2, 0)),
        [sds((width, RECV), BF16)] * 2,
        [SMEM, SMEM, VMEM],
        (*table, home),
        4 * width * WINDOW * RECV,
    )
    frequency = np.exp(-np.log(ROPE_BASE) * np.arange(HALF) / HALF).astype(np.float32)
    frequency = jnp.asarray(np.broadcast_to(frequency[:, None], (HALF, HEAD)))
    tables = call(
        functools.partial(tables_kernel, replicas),
        [sds((HALF, RECV), F32), sds((HALF, RECV), F32), sds((8, RECV), jnp.int32), sds((HEAD, RECV), BF16)],
        [SMEM, SMEM, SMEM, VMEM, VMEM],
        (*table, margins, frequency, grad_attended),
        1000,
    )
    own_w, away_w = call(
        weights_kernel,
        [sds((blocks, width, 2 * HEAD), BF16)] * 2,
        [VMEM, VMEM],
        (q_weight.reshape(blocks, 2, width, HEAD), kv_weight.reshape(blocks, 2, width, HEAD)),
        1000,
    )
    other_w = to_core(away_w)
    bucket = jnp.pad(bucket, ((0, 0), (TAIL, 0))) + second
    bucket, tables, own_w = lax.optimization_barrier((bucket, tables, own_w))
    (turned,) = call(
        turned_kernel,
        [sds((blocks, 4 * HEAD, width), BF16)],
        [VMEM, VMEM],
        (own_w, other_w),
        1000,
    )
    mine = along(bucket, 2) + first + zeroth

    mine_y = to_y(mine)
    near = to_near(mine)
    far = to_far(mine)
    far_y = to_far(mine_y)
    near_y = to_near(mine_y)
    across = to_far(near)
    across_y = to_near(far_y)
    (before,) = call(
        functools.partial(project_kernel, (0, 1, 4, 6)),
        [sds((4 * HEAD, RECV), F32)],
        [VMEM] * 5,
        (turned, mine, near, mine_y, far_y),
        blocks * width * 4 * HEAD * RECV,
    )
    keep, send = call(
        functools.partial(project_last_kernel, (2, 3, 5, 7)),
        [sds((3 * HEAD, RECV), F32), sds((3 * HEAD, RECV), BF16)],
        [VMEM] * 6,
        (turned, before, far, across, near_y, across_y),
        blocks * width * 4 * HEAD * RECV,
    )
    got = of_cores(send)
    attended, send, held = call(
        attention_kernel,
        [sds((RECV, HEAD), BF16), sds((3 * HEAD, RECV), BF16), sds((2 * HEAD, RECV), F32)],
        [VMEM] * 6,
        (keep, got, *tables),
        14 * HEAD * RECV * RECV,
    )
    got = of_cores(send)

    def spread(numbers):
        return call(
            functools.partial(spread_kernel, numbers),
            [sds((width, RECV), BF16)] * len(numbers),
            [VMEM] * 5,
            (own_w, other_w, send, held, got),
            len(numbers) * width * 8 * HEAD * RECV,
        )

    across_y, far, near_y, across = spread((7, 2, 5, 3))
    mine, near, mine_y, far_y = spread((0, 1, 4, 6))
    forward_y = plus(far_y, to_near(across_y))
    forward = plus(near, to_far(across))
    here_y = plus(mine_y, to_near(near_y), to_far(forward_y))
    here = plus(mine, to_far(far), to_near(forward), to_y(here_y))

    back2 = along(here, -2)
    back1 = along(here, -1)
    back3 = along(back2[:, TAIL:], -1)
    most, window = call(
        functools.partial(unpack_kernel, replicas),
        [sds((width, HOME), BF16), sds((width, WINDOW), BF16)],
        [SMEM, SMEM, VMEM, VMEM, VMEM],
        (*table, here, back1, back2),
        6 * width * WINDOW * RECV,
    )
    grad_home = pl.pallas_call(
        functools.partial(unpack_last_kernel, replicas),
        out_shape=sds((width, HOME), BF16),
        in_specs=[SMEM, SMEM, VMEM, VMEM, pl.BlockSpec(memory_space=pl.ANY)],
        out_specs=pl.BlockSpec(memory_space=pl.ANY),
        scratch_shapes=[pltpu.VMEM((width, WINDOW), BF16), pltpu.SemaphoreType.DMA],
        input_output_aliases={4: 0},
        compiler_params=pltpu.CompilerParams(vmem_limit_bytes=24 << 20),
        cost_estimate=pl.CostEstimate(
            flops=2 * width * WINDOW * CAP, bytes_accessed=4 * width * WINDOW, transcendentals=0
        ),
    )(*table, window, back3, most)
    return (attended, grad_home.T)


def solution(mesh):
    return jax.shard_map(
        body,
        mesh=mesh,
        in_specs=(P("dp", "mp"), P(None, "mp"), P(None, "mp"), P(), P(), P(), P("dp", "mp")),
        out_specs=(P("dp", "mp"), P("dp", "mp")),
        check_vma=False,
    )
```

```python
import functools

import jax
import jax.numpy as jnp
import numpy as np
from jax import lax
from jax.experimental import pallas as pl
from jax.experimental.pallas import tpu as pltpu
from jax.sharding import PartitionSpec as P

SPREAD = 4
RECV = 512
CAP = 384
HOME = 1536
TAIL = RECV - CAP
HEAD = 128
HALF = 64
WINDOW = 512

BETA = 0.1
SOFT_CAP = 50.0
ROPE_BASE = 10000.0
QUERY_SCALE = 1.0 / 12.0

F32 = jnp.float32
BF16 = jnp.bfloat16

VMEM = pl.BlockSpec(memory_space=pltpu.VMEM)
SMEM = pl.BlockSpec(memory_space=pltpu.SMEM)
NN = (((1,), (0,)), ((), ()))
NT = (((1,), (1,)), ((), ()))
TN = (((0,), (0,)), ((), ()))


def dot(a, b, dims):
    return lax.dot_general(a, b, dims, preferred_element_type=F32)


def call(kernel, outs, in_specs, args, flops, scratch=(), limit=24):
    moved = sum(int(np.prod(o.shape)) * o.dtype.itemsize for o in outs)
    moved += sum(int(np.prod(a.shape)) * a.dtype.itemsize for a in args)
    return pl.pallas_call(
        kernel,
        out_shape=outs,
        in_specs=in_specs,
        out_specs=[VMEM] * len(outs),
        scratch_shapes=list(scratch),
        compiler_params=pltpu.CompilerParams(vmem_limit_bytes=limit << 20),
        cost_estimate=pl.CostEstimate(flops=flops, bytes_accessed=moved, transcendentals=0),
    )(*args)


def sds(shape, dtype):
    return jax.ShapeDtypeStruct(shape, dtype)


def pair_at(tokens, target, home, replica):
    start, running = jnp.int32(0), jnp.int32(0)
    chosen, rejected, index = jnp.int32(0), jnp.int32(0), jnp.int32(0)
    for p in range(SPREAD):
        i = home * SPREAD + p
        hit = target[i] == replica
        c, r = tokens[0, i], tokens[1, i]
        start = jnp.where(hit, running, start)
        chosen = jnp.where(hit, c, chosen)
        rejected = jnp.where(hit, r, rejected)
        index = jnp.where(hit, i, index)
        running = running + c + r
    return start, chosen, rejected, index


def around(index, count):
    return lax.rem(index + count, count)


def outgoing(tokens, target, replicas, replica, offset):
    there = around(replica + offset, replicas)
    start, chosen, rejected, _ = pair_at(tokens, target, replica, there)
    place = jnp.int32(0)
    for nearer in range(offset):
        _, c, r, _ = pair_at(tokens, target, around(there - nearer, replicas), there)
        place = place + c + r
    return start, chosen + rejected, place


def window_of(start):
    first = jnp.minimum((start // 128) * 128, HOME - WINDOW)
    return pl.multiple_of(first, 128)


def pack_one(replicas, offset, tokens, target, home, out, wait=None):
    replica = lax.axis_index("dp")
    start, size, place = outgoing(tokens, target, replicas, replica, offset)
    first = window_of(start)
    columns = out.shape[1]
    column = lax.broadcasted_iota(jnp.int32, (1, columns), 1) + RECV - columns
    live = (column >= place) & (column < place + size)
    source = jnp.where(live, column - place + start - first, -1)
    row = lax.broadcasted_iota(jnp.int32, (WINDOW, columns), 0)
    pick = jnp.where(row == source, 1.0, 0.0).astype(BF16)
    if wait is not None:
        wait()
    out[...] = dot(home[:, pl.ds(first, WINDOW)], pick, NN).astype(BF16)


def pack_first_kernel(replicas, tokens, target, home, out, tokens_in, target_in, home_in, sems):
    copies = [
        pltpu.make_async_copy(source, place, sems.at[i])
        for i, (source, place) in enumerate(
            ((tokens, tokens_in), (target, target_in), (home, home_in))
        )
    ]
    for copy in copies:
        copy.start()
    copies[0].wait()
    copies[1].wait()
    pack_one(replicas, SPREAD - 1, tokens_in, target_in, home_in, out, copies[2].wait)


def pack_kernel(replicas, offsets, tokens, target, home, *outs):
    for offset, out in zip(offsets, outs):
        pack_one(replicas, offset, tokens, target, home, out)


def weights_kernel(q, kv, own, away):
    core = lax.rem(lax.axis_index("mp"), 2)
    for block in range(q.shape[0]):
        own[block, :, :HEAD] = q[block, core]
        own[block, :, HEAD:] = kv[block, core]
        away[block, :, :HEAD] = q[block, 1 - core]
        away[block, :, HEAD:] = kv[block, 1 - core]


def turned_kernel(own, away, out):
    for block in range(own.shape[0]):
        out[block, : 2 * HEAD] = own[block].astype(F32).T.astype(BF16)
        out[block, 2 * HEAD :] = away[block].astype(F32).T.astype(BF16)


def tables_kernel(replicas, tokens, target, margins, frequency, grad, cosine, sine, begin, upstream):
    replica = lax.axis_index("dp")
    row = lax.broadcasted_iota(jnp.int32, (1, RECV), 1)
    first = jnp.zeros((1, RECV), jnp.int32)
    margin = jnp.zeros((1, RECV), F32)
    sign = jnp.zeros((1, RECV), F32)
    place = jnp.int32(0)
    for offset in range(SPREAD):
        home = around(replica - offset, replicas)
        _, chosen, rejected, index = pair_at(tokens, target, home, replica)
        first = jnp.where(row >= place, place, first)
        margin = jnp.where(row >= place, margins[index], margin)
        sign = jnp.where(row >= place, -1.0, sign)
        first = jnp.where(row >= place + chosen, place + chosen, first)
        sign = jnp.where(row >= place + chosen, 1.0, sign)
        place = place + chosen + rejected
    begin[...] = jnp.broadcast_to(first, begin.shape)
    coef = BETA * sign / (1.0 + jnp.exp(BETA * margin))
    upstream[...] = (grad[...].astype(F32).T * coef).astype(BF16)
    angle = (row - first).astype(F32) * frequency[:, :1]
    cosine[...] = jnp.cos(angle)
    sine[...] = jnp.sin(angle)


def block_index(relative):
    place = lax.axis_index("mp")
    x, y = place // 4, lax.rem(place // 2, 2)
    near, far = x + 1 - 2 * lax.rem(x, 2), 3 - x
    across = far + 1 - 2 * lax.rem(far, 2)
    return (x, near, far, across)[relative % 4] * 2 + (y if relative < 4 else 1 - y)


def partial_products(turned, pieces, numbers):
    total = None
    for relative, piece in zip(numbers, pieces):
        term = dot(turned[block_index(relative)], piece[...], NN)
        total = term if total is None else total + term
    return total


def project_kernel(numbers, turned, *refs):
    pieces, out = refs[:-1], refs[-1]
    out[...] = partial_products(turned, pieces, numbers)


def project_last_kernel(numbers, turned, before, *refs):
    pieces, (keep, send) = refs[:-2], refs[-2:]
    total = before[...] + partial_products(turned, pieces, numbers)
    keep[: 2 * HEAD] = total[: 2 * HEAD]
    keep[2 * HEAD :] = total[3 * HEAD :]
    send[: 2 * HEAD] = total[2 * HEAD :].astype(BF16)
    send[2 * HEAD :] = total[HEAD : 2 * HEAD].astype(BF16)


def turn(value, cosine, sine):
    low, high = value[:HALF], value[HALF:]
    return jnp.concatenate([low * cosine - high * sine, high * cosine + low * sine], axis=0)


def attention_kernel(kept, got, cosine, sine, begin, upstream, attended, send, held):
    core = lax.rem(lax.axis_index("mp"), 2)
    first_core = core == 0
    cos, sin = cosine[...], sine[...]
    total = kept[...] + got[1 - core].astype(F32)
    own, other = total[HEAD : 2 * HEAD], total[2 * HEAD :]
    query = (QUERY_SCALE * turn(total[:HEAD], cos, sin)).astype(BF16)
    key = turn(jnp.where(first_core, own, other), cos, sin).astype(BF16)
    value = jnp.where(first_core, other, own).astype(BF16)
    scores = dot(key, query, TN)
    bent = jnp.tanh(scores / SOFT_CAP)
    key_row = lax.broadcasted_iota(jnp.int32, (RECV, RECV), 0)
    query_row = lax.broadcasted_iota(jnp.int32, (RECV, RECV), 1)
    allowed = (key_row <= query_row) & (key_row >= begin[:1, :])
    exponent = jnp.where(allowed, jnp.exp(SOFT_CAP * bent), 0.0)
    weights = exponent * (1.0 / jnp.sum(exponent, axis=0, keepdims=True))
    probs = weights.astype(BF16)
    attended[...] = dot(value, probs, NN).T.astype(BF16)
    up = upstream[...]
    dprobs = dot(value, up, TN)
    delta = jnp.sum(weights * dprobs, axis=0, keepdims=True)
    dscores = (weights * (dprobs - delta) * (1.0 - bent * bent)).astype(BF16)
    dquery = QUERY_SCALE * turn(dot(key, dscores, NN), cos, -sin)
    dkey = turn(dot(query, dscores, NT), cos, -sin)
    dvalue = dot(up, probs, NT)
    down, dother = jnp.where(first_core, dkey, dvalue), jnp.where(first_core, dvalue, dkey)
    send[:HEAD] = dquery.astype(BF16)
    send[HEAD : 2 * HEAD] = down.astype(BF16)
    send[2 * HEAD :] = dother.astype(BF16)
    held[:HEAD] = down
    held[HEAD:] = dother


def gradients(sent, held, both):
    got = both.at[1 - lax.rem(lax.axis_index("mp"), 2)]
    down = (held[:HEAD] + got[2 * HEAD :].astype(F32)).astype(BF16)
    dother = (held[HEAD:] + got[HEAD : 2 * HEAD].astype(F32)).astype(BF16)
    mine = jnp.concatenate([sent[:HEAD], down], axis=0)
    other = jnp.concatenate([got[:HEAD], dother], axis=0)
    return mine, other


def spread_kernel(numbers, own, away, sent, held, got, *outs):
    mine, other = gradients(sent, held, got)
    for relative, out in zip(numbers, outs):
        block = block_index(relative)
        out[...] = (dot(own[block], mine, NN) + dot(away[block], other, NN)).astype(BF16)


def unpack_one(replicas, offset, tokens, target, piece):
    replica = lax.axis_index("dp")
    start, size, place = outgoing(tokens, target, replicas, replica, offset)
    first = window_of(start)
    columns = piece.shape[1]
    column = lax.broadcasted_iota(jnp.int32, (columns, 1), 0) + RECV - columns
    live = (column >= place) & (column < place + size)
    dest = jnp.where(live, column - place + start - first, -1)
    spot = lax.broadcasted_iota(jnp.int32, (columns, WINDOW), 1)
    pick = jnp.where(spot == dest, 1.0, 0.0).astype(BF16)
    return first, dot(piece[...], pick, NN)


def unpack_kernel(replicas, tokens, target, *refs):
    pieces, (home, last) = refs[:-2], refs[-2:]
    home[...] = jnp.zeros_like(home)
    for offset, piece in enumerate(pieces):
        first, back = unpack_one(replicas, offset, tokens, target, piece)
        window = home[:, pl.ds(first, WINDOW)]
        home[:, pl.ds(first, WINDOW)] = (window.astype(F32) + back).astype(BF16)
    replica = lax.axis_index("dp")
    start, _, _ = outgoing(tokens, target, replicas, replica, SPREAD - 1)
    last[...] = home[:, pl.ds(window_of(start), WINDOW)]


def unpack_last_kernel(replicas, tokens, target, window, piece, home, out, whole, sem):
    first, back = unpack_one(replicas, SPREAD - 1, tokens, target, piece)
    whole[...] = (window[...].astype(F32) + back).astype(BF16)
    copy = pltpu.make_async_copy(whole, out.at[:, pl.ds(first, WINDOW)], sem)
    copy.start()
    copy.wait()


def along(value, steps):
    count = lax.axis_size("dp")
    return lax.ppermute(value, "dp", [(s, (s + steps) % count) for s in range(count)])


def swap(value, change):
    count = lax.axis_size("mp")
    pairs = []
    for source in range(count):
        x, y, core = source // 4, source // 2 % 2, source % 2
        x, y, core = change(x, y, core)
        pairs.append((source, x * 4 + y * 2 + core))
    return lax.ppermute(value, "mp", pairs)


def to_core(value):
    return swap(value, lambda x, y, core: (x, y, 1 - core))


def of_cores(value):
    count = lax.axis_size("mp")
    groups = [[place, place + 1] for place in range(0, count, 2)]
    return lax.all_gather(value, "mp", axis_index_groups=groups)


def to_y(value):
    return swap(value, lambda x, y, core: (x, 1 - y, core))


def to_near(value):
    return swap(value, lambda x, y, core: (x ^ 1, y, core))


def to_far(value):
    return swap(value, lambda x, y, core: (3 - x, y, core))


def plus(*terms):
    return sum(t.astype(F32) for t in terms).astype(BF16)


def body(tokens_home, q_weight, kv_weight, pair_tokens, pair_target, margins, grad_attended):
    replicas = lax.axis_size("dp")
    blocks = lax.axis_size("mp") // 2
    width = tokens_home.shape[1]
    table = (pair_tokens.T, pair_target)
    home = tokens_home.T

    third = pl.pallas_call(
        functools.partial(pack_first_kernel, replicas),
        out_shape=sds((width, CAP), BF16),
        in_specs=[pl.BlockSpec(memory_space=pl.ANY)] * 3,
        out_specs=VMEM,
        scratch_shapes=[
            pltpu.SMEM(table[0].shape, jnp.int32),
            pltpu.SMEM(table[1].shape, jnp.int32),
            pltpu.VMEM(home.shape, BF16),
            pltpu.SemaphoreType.DMA((3,)),
        ],
        compiler_params=pltpu.CompilerParams(vmem_limit_bytes=60 << 20),
        cost_estimate=pl.CostEstimate(
            flops=2 * width * WINDOW * CAP, bytes_accessed=2 * width * HOME, transcendentals=0
        ),
    )(*table, home)
    bucket = along(third, 1)
    (first,) = call(
        functools.partial(pack_kernel, replicas, (1,)),
        [sds((width, RECV), BF16)],
        [SMEM, SMEM, VMEM],
        (*table, home),
        2 * width * WINDOW * RECV,
    )
    first = along(first, 1)
    second, zeroth = call(
        functools.partial(pack_kernel, replicas, (2, 0)),
        [sds((width, RECV), BF16)] * 2,
        [SMEM, SMEM, VMEM],
        (*table, home),
        4 * width * WINDOW * RECV,
    )
    frequency = np.exp(-np.log(ROPE_BASE) * np.arange(HALF) / HALF).astype(np.float32)
    frequency = jnp.asarray(np.broadcast_to(frequency[:, None], (HALF, HEAD)))
    tables = call(
        functools.partial(tables_kernel, replicas),
        [sds((HALF, RECV), F32), sds((HALF, RECV), F32), sds((8, RECV), jnp.int32), sds((HEAD, RECV), BF16)],
        [SMEM, SMEM, SMEM, VMEM, VMEM],
        (*table, margins, frequency, grad_attended),
        1000,
    )
    own_w, away_w = call(
        weights_kernel,
        [sds((blocks, width, 2 * HEAD), BF16)] * 2,
        [VMEM, VMEM],
        (q_weight.reshape(blocks, 2, width, HEAD), kv_weight.reshape(blocks, 2, width, HEAD)),
        1000,
    )
    other_w = to_core(away_w)
    bucket = jnp.pad(bucket, ((0, 0), (TAIL, 0))) + second
    (turned,) = call(
        turned_kernel,
        [sds((blocks, 4 * HEAD, width), BF16)],
        [VMEM, VMEM],
        (own_w, other_w),
        1000,
    )
    mine = along(bucket, 2) + first + zeroth

    mine_y = to_y(mine)
    near = to_near(mine)
    far = to_far(mine)
    far_y = to_far(mine_y)
    near_y = to_near(mine_y)
    across = to_far(near)
    across_y = to_near(far_y)
    (before,) = call(
        functools.partial(project_kernel, (0, 1, 4, 6)),
        [sds((4 * HEAD, RECV), F32)],
        [VMEM] * 5,
        (turned, mine, near, mine_y, far_y),
        blocks * width * 4 * HEAD * RECV,
    )
    keep, send = call(
        functools.partial(project_last_kernel, (2, 3, 5, 7)),
        [sds((3 * HEAD, RECV), F32), sds((3 * HEAD, RECV), BF16)],
        [VMEM] * 6,
        (turned, before, far, across, near_y, across_y),
        blocks * width * 4 * HEAD * RECV,
    )
    got = of_cores(send)
    attended, send, held = call(
        attention_kernel,
        [sds((RECV, HEAD), BF16), sds((3 * HEAD, RECV), BF16), sds((2 * HEAD, RECV), F32)],
        [VMEM] * 6,
        (keep, got, *tables),
        14 * HEAD * RECV * RECV,
    )
    got = of_cores(send)

    def spread(numbers):
        return call(
            functools.partial(spread_kernel, numbers),
            [sds((width, RECV), BF16)] * len(numbers),
            [VMEM] * 5,
            (own_w, other_w, send, held, got),
            len(numbers) * width * 8 * HEAD * RECV,
        )

    across_y, far, near_y, across = spread((7, 2, 5, 3))
    mine, near, mine_y, far_y = spread((0, 1, 4, 6))
    forward_y = plus(far_y, to_near(across_y))
    forward = plus(near, to_far(across))
    here_y = plus(mine_y, to_near(near_y), to_far(forward_y))
    here = plus(mine, to_far(far), to_near(forward), to_y(here_y))

    back2 = along(here, -2)
    back1 = along(here, -1)
    back3 = along(back2[:, TAIL:], -1)
    most, window = call(
        functools.partial(unpack_kernel, replicas),
        [sds((width, HOME), BF16), sds((width, WINDOW), BF16)],
        [SMEM, SMEM, VMEM, VMEM, VMEM],
        (*table, here, back1, back2),
        6 * width * WINDOW * RECV,
    )
    grad_home = pl.pallas_call(
        functools.partial(unpack_last_kernel, replicas),
        out_shape=sds((width, HOME), BF16),
        in_specs=[SMEM, SMEM, VMEM, VMEM, pl.BlockSpec(memory_space=pl.ANY)],
        out_specs=pl.BlockSpec(memory_space=pl.ANY),
        scratch_shapes=[pltpu.VMEM((width, WINDOW), BF16), pltpu.SemaphoreType.DMA],
        input_output_aliases={4: 0},
        compiler_params=pltpu.CompilerParams(vmem_limit_bytes=24 << 20),
        cost_estimate=pl.CostEstimate(
            flops=2 * width * WINDOW * CAP, bytes_accessed=4 * width * WINDOW, transcendentals=0
        ),
    )(*table, window, back3, most)
    return (attended, grad_home.T)


def solution(mesh):
    return jax.shard_map(
        body,
        mesh=mesh,
        in_specs=(P("dp", "mp"), P(None, "mp"), P(None, "mp"), P(), P(), P(), P("dp", "mp")),
        out_specs=(P("dp", "mp"), P("dp", "mp")),
        check_vma=False,
    )
```
